32 devices in a mesh: group: 2 (over y), atom: 8 (over z, x), wave: 2 (over core).
Axes of the slice: x: 2, y: 2, z: 4, core: 2. Of those that a mesh axis runs over, the one named last changes fastest.
Arguments:
- positions: float32 [3, 16384], P(None, ('group', 'atom')), parts along dimension 1, may hold values from 0 to 64
- features: bfloat16 [16384, 256], P(('group', 'atom')), parts along dimension 0, may hold values from -6 to 6
- cotangent: bfloat16 [16384, 256], P(('group', 'atom')), parts along dimension 0, may hold values from -6 to 6
- filters: float32 [4096, 256], P('wave'), may hold values from -12 to 12
- wave_ints: int32 [3, 4096], P(None, 'wave'), may hold values from -12 to 12, as said below
Outputs:
- grad_features: float32 [16384, 256], P(('group', 'atom', 'wave')), parts along dimension 0
- grad_positions: float32 [3, 16384], P(None, ('group', 'atom', 'wave')), parts along dimension 1
- grad_filter: float32 [8192, 256], P(('group', 'wave')), parts along dimension 0
The draws below stay inside these ranges and needn't reach their ends.
There are 2 independent parts, one for each index of `group`. The reference program is written for one: setup_inputs(seed, part) draws one part's arguments, and reference() takes and returns one part's arrays. A program takes and returns all parts, laid end to end along the dimension named above; an argument that names none is the same for every part. Nothing has to cross between parts.
Inputs may be any that keep to these rules, and one draw needn't show every extreme that they name: `wave_ints`: the 4096 index triples are distinct and nonzero, and all lie in one half-space: first component positive, or first component zero and second positive, or the first two zero and the third positive; so no wavevector appears together with its negative.
All inputs are finite; a program needn't handle non-finite values.
Results may differ from the reference program's by a relative error of at most 0.0047.
Values may be sent and summed in bfloat16 or wider, within the bound.
A program may use at most 128 MiB of HBM per device.

```python
import math
import jax
import jax.numpy as jnp
import numpy as np
from jax import lax

F = 256
K = 4096
BOX = 64
ATOM_DEV = 1024
ATOMS = 8192


def half_space_vectors():
    extent = np.arange(-12, 13)
    grid_x, grid_y, grid_z = np.meshgrid(extent, extent, extent, indexing='ij')
    inside = (grid_x > 0) | (grid_x == 0) & (grid_y > 0) | (grid_x == 0) & (grid_y == 0) & (grid_z > 0)
    return np.stack([grid_x[inside], grid_y[inside], grid_z[inside]]).astype(np.int32)


def draw_wave_ints(key, part):
    candidates = jnp.asarray(half_space_vectors())
    shuffled = jax.random.permutation(key, candidates.shape[1])
    return candidates[:, shuffled[:K]]


def levels(key, shape, cuts, low, largest):
    gain, own = 1.0, jax.random.fold_in(key, 6)
    for position, shards_of in cuts:
        draws = jnp.exp(jax.random.uniform(jax.random.fold_in(own, position), (shards_of,), jnp.float32, low / len(cuts), largest / len(cuts)))
        gain = gain * jnp.repeat(draws, shape[position] // shards_of).reshape([-1 if axis == position else 1 for axis in range(len(shape))])
    return gain


def noise(rng, shape, scale, limit, split=(), held_as=jnp.bfloat16):
    gain = levels(rng, shape, split, -0.22, 0.18) if split else 1.0
    result = jax.random.normal(rng, shape, jnp.float32) * scale * gain
    return jnp.minimum(jnp.maximum(result, -limit), limit).astype(held_as)


def setup_inputs(seed: int = 0, part: int = 0) -> dict:
    keys = jax.random.split(jax.random.key(seed), 6)
    part_splits = jax.random.split(jax.random.fold_in(keys[5], part), 6)
    return {
        "positions": jnp.clip(64.0 * jax.random.uniform(part_splits[0], (3, ATOMS), jnp.float32) ** levels(part_splits[0], (3, ATOMS), ((1, 8),), -0.2, 0.2), 0.0, 64.0),
        "features": noise(part_splits[1], (ATOMS, F), 1.0, 6.0, ((0, 8),)),
        "cotangent": noise(part_splits[2], (ATOMS, F), 1.0, 6.0, ((0, 8),)),
        "filters": noise(keys[3], (K, F), 2.0, 12.0, ((0, 2),), jnp.float32),
        "wave_ints": draw_wave_ints(jax.random.fold_in(keys[5], 71), part),
    }


def phase_tiles(block_pos, waves):
    theta = (block_pos[0][:, None] * waves[0][None, :] + block_pos[1][:, None] * waves[1][None, :]
             + block_pos[2][:, None] * waves[2][None, :])
    theta = (2.0 * math.pi / BOX) * theta
    return jnp.cos(theta), jnp.sin(theta)


def reference(positions, features, cotangent, filters, wave_ints):
    waves = wave_ints.astype(jnp.float32)
    waves_half = wave_ints.astype(jnp.bfloat16)
    count = positions.shape[1] // ATOM_DEV
    pos_blocks = positions.reshape(3, count, ATOM_DEV).transpose(1, 0, 2)
    feat_blocks = features.reshape(count, ATOM_DEV, F)
    cot_blocks = cotangent.reshape(count, ATOM_DEV, F)

    def accumulate(carry, items):
        block_pos, feats, cots = items
        cosine, sine = phase_tiles(block_pos, waves)
        cos_half = cosine.astype(jnp.bfloat16)
        sin_half = sine.astype(jnp.bfloat16)
        return (carry[0] + jnp.dot(cos_half.T, feats, preferred_element_type=jnp.float32),
                carry[1] + jnp.dot(sin_half.T, feats, preferred_element_type=jnp.float32),
                carry[2] + jnp.dot(cos_half.T, cots, preferred_element_type=jnp.float32),
                carry[3] + jnp.dot(sin_half.T, cots, preferred_element_type=jnp.float32)), None

    zeros = jnp.zeros((K, F), jnp.float32)
    (s_cos, s_sin, a_cos, a_sin), _ = lax.scan(accumulate, (zeros, zeros, zeros, zeros), (pos_blocks, feat_blocks, cot_blocks))
    grad_filter = (s_cos * a_cos + s_sin * a_sin) / ATOMS
    f_sc = (filters * s_cos / ATOMS).astype(jnp.bfloat16)
    f_ss = (filters * s_sin / ATOMS).astype(jnp.bfloat16)
    f_ac = (filters * a_cos / ATOMS).astype(jnp.bfloat16)
    f_as = (filters * a_sin / ATOMS).astype(jnp.bfloat16)

    def backward(items):
        block_pos, feats, cots = items
        cosine, sine = phase_tiles(block_pos, waves)
        cos_half = cosine.astype(jnp.bfloat16)
        sin_half = sine.astype(jnp.bfloat16)
        grad_feat = jnp.dot(cos_half, f_ac, preferred_element_type=jnp.float32) + jnp.dot(sin_half, f_as, preferred_element_type=jnp.float32)
        pcoef = jnp.dot(cots, f_sc.T, preferred_element_type=jnp.float32) + jnp.dot(feats, f_ac.T, preferred_element_type=jnp.float32)
        qcoef = jnp.dot(cots, f_ss.T, preferred_element_type=jnp.float32) + jnp.dot(feats, f_as.T, preferred_element_type=jnp.float32)
        dtheta_half = (cosine * qcoef - sine * pcoef).astype(jnp.bfloat16)
        grad_pos = (2.0 * math.pi / BOX) * jnp.dot(waves_half, dtheta_half.T, preferred_element_type=jnp.float32)
        return grad_feat, grad_pos

    grad_feats, grad_poss = lax.map(backward, (pos_blocks, feat_blocks, cot_blocks))
    grad_features = grad_feats.reshape(count * ATOM_DEV, F)
    grad_positions = grad_poss.transpose(1, 0, 2).reshape(3, count * ATOM_DEV)
    return grad_features, grad_positions, grad_filter
```

```python
import functools
import math

import jax
import jax.numpy as jnp
from jax import lax
from jax.experimental import pallas as pl
from jax.experimental.pallas import tpu as pltpu
from jax.sharding import PartitionSpec as P

BOX = 64
TILE = 256
SIN = (6.2831853, -41.3417004, 81.6051314, -76.7030154, 42.025927, -14.8998467, 3.23813751)
COS = (0.999999989, -19.7392045, 64.9391175, -85.4501395, 60.167631, -25.9675992, 6.52865816)


def horner(coeffs, u):
    total = coeffs[-1] * u + coeffs[-2]
    for c in coeffs[-3::-1]:
        total = total * u + c
    return total


def over(a, b, dims):
    return lax.dot_general(a, b, (dims, ((), ())), preferred_element_type=jnp.float32)


def kernel(
    n, parts, total_atoms,
    pos_ref, feat_ref, cot_ref, filt_ref, wcol_ref, wrow_ref,
    gfeat_ref, gpos_ref, gfilt_ref,
    cos_s, sin_s, src, recv, staged, full, grad_t, grad, grad_in, gp, gp_out, gp_in,
    rs_send, rs_recv, ag_send, ag_recv, w_send, w_recv,
):
    stages = n.bit_length() - 1
    waves = filt_ref.shape[0]
    atoms = feat_ref.shape[0]
    rows = waves // parts
    half = atoms // 2
    me = lax.axis_index("atom")
    core = lax.axis_index("wave")
    bits = [lax.rem(me // (1 << b), 2) for b in range(stages)]
    partners = [me + (1 - 2 * bits[b]) * (1 << b) for b in range(stages)]

    barrier = pltpu.get_barrier_semaphore()
    for partner in partners:
        pl.semaphore_signal(
            barrier, inc=1, device_id={"atom": partner}, device_id_type=pl.DeviceIdType.MESH
        )
    pl.semaphore_signal(
        barrier, inc=1, device_id={"wave": 1 - core}, device_id_type=pl.DeviceIdType.MESH
    )

    def order(p):
        return list(range(stages)) if p % 2 == 0 else list(range(1, stages)) + [0]

    def region(p, s):
        return p * rows + rows - (rows >> s)

    def remote(src_ref, dst_ref, send, recv_sem, axis, target):
        return pltpu.make_async_remote_copy(
            src_ref=src_ref, dst_ref=dst_ref, send_sem=send, recv_sem=recv_sem,
            device_id={axis: target}, device_id_type=pl.DeviceIdType.MESH,
        )

    def scatter_copy(p, s):
        where = pl.ds(region(p, s), rows >> (s + 1))
        return remote(
            staged.at[where], recv.at[where],
            rs_send.at[p * stages + s], rs_recv.at[p * stages + s], "atom",
            partners[order(p)[s]],
        )

    def stage(p, s):
        size = rows >> (s + 1)
        base = p * rows if s == 0 else offset(p, s - 1)
        start = base + (1 - bits[order(p)[s]]) * size
        step = min(size, 32)

        def narrow(i, _):
            a = src[pl.ds(pl.multiple_of(start + i * step, 16), step), :]
            to = pl.ds(pl.multiple_of(region(p, s) + i * step, 16), step)
            staged[to, :] = a.astype(jnp.bfloat16)
            return 0

        lax.fori_loop(0, size // step, narrow, 0)

    def offset(p, s):
        off = p * rows
        for j in range(s + 1):
            off = off + bits[order(p)[j]] * (rows >> (j + 1))
        return pl.multiple_of(off, 16)

    def gather_copy(p, s):
        size = rows >> (s + 1)
        where = pl.ds(offset(p, s), size)
        return remote(
            full.at[where], full.at[where],
            ag_send.at[p * stages + s], ag_recv.at[p * stages + s], "atom",
            partners[order(p)[s]],
        )

    p0 = pos_ref[0:1, :]
    p1 = pos_ref[1:2, :]
    p2 = pos_ref[2:3, :]

    def phase(i, _):
        at = pl.ds(pl.multiple_of(i * 16, 16), 16)
        w = wcol_ref[at, :]
        turns = w[:, 0:1] * p0 + w[:, 1:2] * p1 + w[:, 2:3] * p2
        frac = turns - jnp.round(turns)
        u = frac * frac
        sin_s[at, :] = horner(SIN, u) * frac
        cos_s[at, :] = horner(COS, u)
        return 0

    def forward(j, _):
        lax.fori_loop(j * (TILE // 16), (j + 1) * (TILE // 16), phase, 0)
        at = pl.ds(pl.multiple_of(j * TILE, TILE), TILE)
        channels = feat_ref.shape[1]
        c = cos_s[at, :].astype(jnp.bfloat16)
        s = sin_s[at, :].astype(jnp.bfloat16)
        nn = ((1,), (0,))
        for k, (wave, data) in enumerate(
            ((c, feat_ref), (s, feat_ref), (c, cot_ref), (s, cot_ref))
        ):
            src[at, k * channels:(k + 1) * channels] = over(wave, data[...], nn)
        return 0

    def backward(j, _):
        at = pl.ds(pl.multiple_of(j * TILE, TILE), TILE)
        channels = feat_ref.shape[1]
        s_cos, s_sin, a_cos, a_sin = [
            full[at, k * channels:(k + 1) * channels].astype(jnp.float32) for k in range(4)
        ]
        gfilt_ref[at, :] = (s_cos * a_cos + s_sin * a_sin) * (1.0 / total_atoms)
        filt = filt_ref[at, :] * (1.0 / total_atoms)
        f_sc = (filt * s_cos).astype(jnp.bfloat16)
        f_ss = (filt * s_sin).astype(jnp.bfloat16)
        f_ac = (filt * a_cos).astype(jnp.bfloat16)
        f_as = (filt * a_sin).astype(jnp.bfloat16)
        c = cos_s[at, :].astype(jnp.bfloat16)
        s = sin_s[at, :].astype(jnp.bfloat16)
        nt = ((1,), (1,))
        tn = ((0,), (0,))
        grad_t[...] += over(f_ac, c, tn) + over(f_as, s, tn)
        for h in range(2):
            cut = slice(h * half, (h + 1) * half)
            cot = cot_ref[cut, :]
            feat = feat_ref[cut, :]
            pcoef = over(f_sc, cot, nt) + over(f_ac, feat, nt)
            qcoef = over(f_ss, cot, nt) + over(f_as, feat, nt)
            dtheta = (
                cos_s[at, cut] * qcoef
                - sin_s[at, cut] * pcoef
            ).astype(jnp.bfloat16)
            gp[h] += over(wrow_ref[j], dtheta, ((1,), (0,)))
        return 0

    tiles = rows // TILE
    copies = []
    for p in range(parts):
        lax.fori_loop(p * tiles, (p + 1) * tiles, forward, 0)
        if p == 0:
            pl.semaphore_wait(barrier, stages + 1)
        stage(p, 0)
        copy = scatter_copy(p, 0)
        copy.start()
        copies.append(copy)
    grad_t[...] = jnp.zeros_like(grad_t)
    gp[...] = jnp.zeros_like(gp)

    for s in range(stages):
        for p in range(parts):
            scatter_copy(p, s).wait_recv()
            size = rows >> (s + 1)
            last = s == stages - 1
            mine = offset(p, s)
            step = min(size, 32)

            def add(i, _, mine=mine, last=last, step=step, came=region(p, s)):
                at = pl.ds(pl.multiple_of(mine + i * step, 16), step)
                b = recv[pl.ds(pl.multiple_of(came + i * step, 16), step), :]
                total = src[at, :] + b.astype(jnp.float32)
                if last:
                    full[at, :] = total.astype(jnp.bfloat16)
                else:
                    src[at, :] = total
                return 0

            lax.fori_loop(0, size // step, add, 0)
            if not last:
                stage(p, s + 1)
            copy = gather_copy(p, s) if last else scatter_copy(p, s + 1)
            copy.start()
            copies.append(copy)

    for s in reversed(range(stages)):
        for p in range(parts):
            gather_copy(p, s).wait_recv()
            if s > 0:
                copy = gather_copy(p, s - 1)
                copy.start()
                copies.append(copy)
            else:
                lax.fori_loop(p * tiles, (p + 1) * tiles, backward, 0)

    grad[...] = grad_t[...].T
    factor = 2.0 * math.pi / BOX
    gp_out[...] = gp[...] * factor
    other = pl.multiple_of((1 - core) * half, half)
    own = pl.multiple_of(core * half, half)
    give = remote(
        grad.at[pl.ds(other, half)], grad_in, w_send.at[0], w_recv.at[0], "wave", 1 - core
    )
    give_pos = remote(
        gp_out.at[1 - core], gp_in, w_send.at[1], w_recv.at[1], "wave", 1 - core
    )
    give.start()
    give_pos.start()
    for copy in copies:
        copy.wait_send()
    give.wait_recv()
    give_pos.wait_recv()
    gfeat_ref[...] = grad[pl.ds(own, half), :] + grad_in[...]
    gpos_ref[...] = gp_out[core] + gp_in[...]
    give.wait_send()
    give_pos.wait_send()


def per_device(positions, features, cotangent, filters, wave_ints):
    n = lax.axis_size("atom")
    atoms, channels = features.shape
    waves = filters.shape[0]
    stages = n.bit_length() - 1
    parts = max(1, min(4, waves // (16 * n)))
    total_atoms = atoms * n
    half = atoms // 2
    scaled = positions * (1.0 / BOX)
    columns = wave_ints.astype(jnp.float32).T
    triples = jnp.pad(wave_ints.astype(jnp.bfloat16), ((0, 13), (0, 0)))
    triples = triples.reshape(16, waves // TILE, TILE).transpose(1, 0, 2)
    vmem = pl.BlockSpec(memory_space=pltpu.VMEM)
    bf16, f32 = jnp.bfloat16, jnp.float32
    count = parts * stages
    grad_features, grad_positions, grad_filter = pl.pallas_call(
        functools.partial(kernel, n, parts, total_atoms),
        out_shape=(
            jax.ShapeDtypeStruct((half, channels), f32),
            jax.ShapeDtypeStruct((16, half), f32),
            jax.ShapeDtypeStruct((waves, channels), f32),
        ),
        in_specs=[vmem] * 6,
        out_specs=(vmem, vmem, vmem),
        scratch_shapes=[
            pltpu.VMEM((waves, atoms), f32),
            pltpu.VMEM((waves, atoms), f32),
            pltpu.VMEM((waves, 4 * channels), f32),
            pltpu.VMEM((waves, 4 * channels), bf16),
            pltpu.VMEM((waves, 4 * channels), bf16),
            pltpu.VMEM((waves, 4 * channels), bf16),
            pltpu.VMEM((channels, atoms), f32),
            pltpu.VMEM((atoms, channels), f32),
            pltpu.VMEM((half, channels), f32),
            pltpu.VMEM((2, 16, half), f32),
            pltpu.VMEM((2, 16, half), f32),
            pltpu.VMEM((16, half), f32),
            pltpu.SemaphoreType.DMA((count,)),
            pltpu.SemaphoreType.DMA((count,)),
            pltpu.SemaphoreType.DMA((count,)),
            pltpu.SemaphoreType.DMA((count,)),
            pltpu.SemaphoreType.DMA((2,)),
            pltpu.SemaphoreType.DMA((2,)),
        ],
        compiler_params=pltpu.CompilerParams(
            collective_id=0, has_side_effects=True, vmem_limit_bytes=56 * 1024 * 1024
        ),
    )(scaled, features, cotangent, filters, columns, triples)
    return (grad_features, grad_positions[:3], grad_filter)


def solution(mesh):
    placed = (
        P(None, ("group", "atom")),
        P(("group", "atom"), None),
        P(("group", "atom"), None),
        P("wave", None),
        P(None, "wave"),
    )
    return jax.shard_map(
        per_device,
        mesh=mesh,
        in_specs=placed,
        out_specs=(
            P(("group", "atom", "wave"), None),
            P(None, ("group", "atom", "wave")),
            P(("group", "wave"), None),
        ),
        check_vma=False,
    )
```

```python
import functools
import math

import jax
import jax.numpy as jnp
from jax import lax
from jax.experimental import pallas as pl
from jax.experimental.pallas import tpu as pltpu
from jax.sharding import PartitionSpec as P

BOX = 64
TILE = 256
SIN = (6.2831853, -41.3417004, 81.6051314, -76.7030154, 42.025927, -14.8998467, 3.23813751)
COS = (0.999999989, -19.7392045, 64.9391175, -85.4501395, 60.167631, -25.9675992, 6.52865816)


def horner(coeffs, u):
    total = coeffs[-1] * u + coeffs[-2]
    for c in coeffs[-3::-1]:
        total = total * u + c
    return total


def over(a, b, dims):
    return lax.dot_general(a, b, (dims, ((), ())), preferred_element_type=jnp.float32)


def kernel(
    n, parts, total_atoms,
    pos_ref, feat_ref, cot_ref, filt_ref, wcol_ref, wrow_ref,
    gfeat_ref, gpos_ref, gfilt_ref,
    cos_s, sin_s, src, recv, staged, full, grad_t, grad, grad_in, gp, gp_out, gp_in,
    rs_send, rs_recv, ag_send, ag_recv, w_send, w_recv,
):
    stages = n.bit_length() - 1
    waves = filt_ref.shape[0]
    atoms = feat_ref.shape[0]
    rows = waves // parts
    half = atoms // 2
    me = lax.axis_index("atom")
    core = lax.axis_index("wave")
    bits = [lax.rem(me // (1 << b), 2) for b in range(stages)]
    partners = [me + (1 - 2 * bits[b]) * (1 << b) for b in range(stages)]

    barrier = pltpu.get_barrier_semaphore()
    for partner in partners:
        pl.semaphore_signal(
            barrier, inc=1, device_id={"atom": partner}, device_id_type=pl.DeviceIdType.MESH
        )
    pl.semaphore_signal(
        barrier, inc=1, device_id={"wave": 1 - core}, device_id_type=pl.DeviceIdType.MESH
    )

    def order(p):
        return list(range(stages)) if p % 2 == 0 else list(range(1, stages)) + [0]

    def region(p, s):
        return p * rows + rows - (rows >> s)

    def remote(src_ref, dst_ref, send, recv_sem, axis, target):
        return pltpu.make_async_remote_copy(
            src_ref=src_ref, dst_ref=dst_ref, send_sem=send, recv_sem=recv_sem,
            device_id={axis: target}, device_id_type=pl.DeviceIdType.MESH,
        )

    def scatter_copy(p, s):
        where = pl.ds(region(p, s), rows >> (s + 1))
        return remote(
            staged.at[where], recv.at[where],
            rs_send.at[p * stages + s], rs_recv.at[p * stages + s], "atom",
            partners[order(p)[s]],
        )

    def stage(p, s):
        size = rows >> (s + 1)
        base = p * rows if s == 0 else offset(p, s - 1)
        start = base + (1 - bits[order(p)[s]]) * size
        step = min(size, 32)

        def narrow(i, _):
            a = src[pl.ds(pl.multiple_of(start + i * step, 16), step), :]
            to = pl.ds(pl.multiple_of(region(p, s) + i * step, 16), step)
            staged[to, :] = a.astype(jnp.bfloat16)
            return 0

        lax.fori_loop(0, size // step, narrow, 0)

    def offset(p, s):
        off = p * rows
        for j in range(s + 1):
            off = off + bits[order(p)[j]] * (rows >> (j + 1))
        return pl.multiple_of(off, 16)

    def gather_copy(p, s):
        size = rows >> (s + 1)
        where = pl.ds(offset(p, s), size)
        return remote(
            full.at[where], full.at[where],
            ag_send.at[p * stages + s], ag_recv.at[p * stages + s], "atom",
            partners[order(p)[s]],
        )

    p0 = pos_ref[0:1, :]
    p1 = pos_ref[1:2, :]
    p2 = pos_ref[2:3, :]

    def phase(i, _):
        at = pl.ds(pl.multiple_of(i * 16, 16), 16)
        w = wcol_ref[at, :]
        turns = w[:, 0:1] * p0 + w[:, 1:2] * p1 + w[:, 2:3] * p2
        frac = turns - jnp.round(turns)
        u = frac * frac
        sin_s[at, :] = horner(SIN, u) * frac
        cos_s[at, :] = horner(COS, u)
        return 0

    def forward(j, _):
        lax.fori_loop(j * (TILE // 16), (j + 1) * (TILE // 16), phase, 0)
        at = pl.ds(pl.multiple_of(j * TILE, TILE), TILE)
        channels = feat_ref.shape[1]
        c = cos_s[at, :].astype(jnp.bfloat16)
        s = sin_s[at, :].astype(jnp.bfloat16)
        nn = ((1,), (0,))
        for k, (wave, data) in enumerate(
            ((c, feat_ref), (s, feat_ref), (c, cot_ref), (s, cot_ref))
        ):
            src[at, k * channels:(k + 1) * channels] = over(wave, data[...], nn)
        return 0

    def backward(j, _):
        at = pl.ds(pl.multiple_of(j * TILE, TILE), TILE)
        channels = feat_ref.shape[1]
        s_cos, s_sin, a_cos, a_sin = [
            full[at, k * channels:(k + 1) * channels].astype(jnp.float32) for k in range(4)
        ]
        gfilt_ref[at, :] = (s_cos * a_cos + s_sin * a_sin) * (1.0 / total_atoms)
        filt = filt_ref[at, :] * (1.0 / total_atoms)
        f_sc = (filt * s_cos).astype(jnp.bfloat16)
        f_ss = (filt * s_sin).astype(jnp.bfloat16)
        f_ac = (filt * a_cos).astype(jnp.bfloat16)
        f_as = (filt * a_sin).astype(jnp.bfloat16)
        c = cos_s[at, :].astype(jnp.bfloat16)
        s = sin_s[at, :].astype(jnp.bfloat16)
        nt = ((1,), (1,))
        tn = ((0,), (0,))
        grad_t[...] += over(f_ac, c, tn) + over(f_as, s, tn)
        for h in range(2):
            cut = slice(h * half, (h + 1) * half)
            cot = cot_ref[cut, :]
            feat = feat_ref[cut, :]
            pcoef = over(f_sc, cot, nt) + over(f_ac, feat, nt)
            qcoef = over(f_ss, cot, nt) + over(f_as, feat, nt)
            dtheta = (
                cos_s[at, cut] * qcoef
                - sin_s[at, cut] * pcoef
            ).astype(jnp.bfloat16)
            gp[h] += over(wrow_ref[j], dtheta, ((1,), (0,)))
        return 0

    tiles = rows // TILE
    copies = []
    for p in range(parts):
        lax.fori_loop(p * tiles, (p + 1) * tiles, forward, 0)
        if p == 0:
            pl.semaphore_wait(barrier, stages + 1)
        stage(p, 0)
        copy = scatter_copy(p, 0)
        copy.start()
        copies.append(copy)
    grad_t[...] = jnp.zeros_like(grad_t)
    gp[...] = jnp.zeros_like(gp)

    for s in range(stages):
        for p in range(parts):
            scatter_copy(p, s).wait_recv()
            size = rows >> (s + 1)
            last = s == stages - 1
            mine = offset(p, s)
            step = min(size, 32)

            def add(i, _, mine=mine, last=last, step=step, came=region(p, s)):
                at = pl.ds(pl.multiple_of(mine + i * step, 16), step)
                b = recv[pl.ds(pl.multiple_of(came + i * step, 16), step), :]
                total = src[at, :] + b.astype(jnp.float32)
                if last:
                    full[at, :] = total.astype(jnp.bfloat16)
                else:
                    src[at, :] = total
                return 0

            lax.fori_loop(0, size // step, add, 0)
            if not last:
                stage(p, s + 1)
            copy = gather_copy(p, s) if last else scatter_copy(p, s + 1)
            copy.start()
            copies.append(copy)

    for s in reversed(range(stages)):
        for p in range(parts):
            gather_copy(p, s).wait_recv()
            if s > 0:
                copy = gather_copy(p, s - 1)
                copy.start()
                copies.append(copy)
            else:
                lax.fori_loop(p * tiles, (p + 1) * tiles, backward, 0)

    grad[...] = grad_t[...].T
    factor = 2.0 * math.pi / BOX
    gp_out[...] = gp[...] * factor
    other = pl.multiple_of((1 - core) * half, half)
    own = pl.multiple_of(core * half, half)
    give = remote(
        grad.at[pl.ds(other, half)], grad_in, w_send.at[0], w_recv.at[0], "wave", 1 - core
    )
    give_pos = remote(
        gp_out.at[1 - core], gp_in, w_send.at[1], w_recv.at[1], "wave", 1 - core
    )
    give.start()
    give_pos.start()
    for copy in copies:
        copy.wait_send()
    give.wait_recv()
    give_pos.wait_recv()
    gfeat_ref[...] = grad[pl.ds(own, half), :] + grad_in[...]
    gpos_ref[...] = gp_out[core] + gp_in[...]
    give.wait_send()
    give_pos.wait_send()


def per_device(positions, features, cotangent, filters, wave_ints):
    n = lax.axis_size("atom")
    atoms, channels = features.shape
    waves = filters.shape[0]
    stages = n.bit_length() - 1
    parts = max(1, min(8, waves // (16 * n)))
    total_atoms = atoms * n
    half = atoms // 2
    scaled = positions * (1.0 / BOX)
    columns = wave_ints.astype(jnp.float32).T
    triples = jnp.pad(wave_ints.astype(jnp.bfloat16), ((0, 13), (0, 0)))
    triples = triples.reshape(16, waves // TILE, TILE).transpose(1, 0, 2)
    vmem = pl.BlockSpec(memory_space=pltpu.VMEM)
    bf16, f32 = jnp.bfloat16, jnp.float32
    count = parts * stages
    grad_features, grad_positions, grad_filter = pl.pallas_call(
        functools.partial(kernel, n, parts, total_atoms),
        out_shape=(
            jax.ShapeDtypeStruct((half, channels), f32),
            jax.ShapeDtypeStruct((16, half), f32),
            jax.ShapeDtypeStruct((waves, channels), f32),
        ),
        in_specs=[vmem] * 6,
        out_specs=(vmem, vmem, vmem),
        scratch_shapes=[
            pltpu.VMEM((waves, atoms), f32),
            pltpu.VMEM((waves, atoms), f32),
            pltpu.VMEM((waves, 4 * channels), f32),
            pltpu.VMEM((waves, 4 * channels), bf16),
            pltpu.VMEM((waves, 4 * channels), bf16),
            pltpu.VMEM((waves, 4 * channels), bf16),
            pltpu.VMEM((channels, atoms), f32),
            pltpu.VMEM((atoms, channels), f32),
            pltpu.VMEM((half, channels), f32),
            pltpu.VMEM((2, 16, half), f32),
            pltpu.VMEM((2, 16, half), f32),
            pltpu.VMEM((16, half), f32),
            pltpu.SemaphoreType.DMA((count,)),
            pltpu.SemaphoreType.DMA((count,)),
            pltpu.SemaphoreType.DMA((count,)),
            pltpu.SemaphoreType.DMA((count,)),
            pltpu.SemaphoreType.DMA((2,)),
            pltpu.SemaphoreType.DMA((2,)),
        ],
        compiler_params=pltpu.CompilerParams(
            collective_id=0, has_side_effects=True, vmem_limit_bytes=56 * 1024 * 1024
        ),
    )(scaled, features, cotangent, filters, columns, triples)
    return (grad_features, grad_positions[:3], grad_filter)


def solution(mesh):
    placed = (
        P(None, ("group", "atom")),
        P(("group", "atom"), None),
        P(("group", "atom"), None),
        P("wave", None),
        P(None, "wave"),
    )
    return jax.shard_map(
        per_device,
        mesh=mesh,
        in_specs=placed,
        out_specs=(
            P(("group", "atom", "wave"), None),
            P(None, ("group", "atom", "wave")),
            P(("group", "wave"), None),
        ),
        check_vma=False,
    )
```
